256 devices in a mesh: replica: 4 (over x_lo, core), dp: 2 (over x_hi), expert: 32 (over z, y).
Axes of the slice: x: 4 (x_hi: 2, x_lo: 2; x = x_hi * 2 + x_lo), y: 4, z: 8, core: 2. Of those that a mesh axis runs over, the one named last changes fastest.
Arguments:
- cotangent: bfloat16 [4, 8192, 3584], P('replica', ('dp', 'expert')), may hold values from -0.59765625 to 0.59765625
- route_weights: float32 [4, 8192, 8], P('replica', ('dp', 'expert')), may hold values from 0.05 to 0.5
- expert_ids: int32 [4, 8192, 8], P('replica', ('dp', 'expert')), may hold values from 0 to 31, all different within a row; in each aligned block of 128 rows (0 to 127, 128 to 255, ..., all dimensions but the last counted through in order) at most 40 rows name the same one
- hidden: bfloat16 [4, 32, 2560, 1024], P('replica', 'expert', 'dp'), may hold values from -6 to 6
- local_fragment: bfloat16 [4, 1024, 3584], P('replica', ('dp', 'expert')), may hold values from -6 to 6
- global_fragment: float32 [1024, 3584], P(('dp', 'expert')), may hold values from -6 to 6
- outer_momentum: float32 [1024, 3584], P(('dp', 'expert')), may hold values from -3 to 3
Outputs:
- expert_grad: bfloat16 [4, 32, 1024, 3584], P('replica', 'expert', None, 'dp')
- new_global: float32 [1024, 3584], P(('dp', 'expert'))
- new_momentum: float32 [1024, 3584], P(('dp', 'expert'))
- mixed_local: bfloat16 [4, 1024, 3584], P('replica', ('dp', 'expert'))
The draws below stay inside these ranges and needn't reach their ends.
Inputs may be any that keep to these rules, and one draw needn't show every extreme that they name: `expert_ids`: each token names 8 different experts; in each aligned block of 128 tokens (the tokens of one device) no expert is named more than 40 times.
All inputs are finite; a program needn't handle non-finite values.
Results may differ from the reference program's by a relative error of at most 0.0049.
Values may be sent and summed in bfloat16 or wider, within the bound.
No kernel may reach another device: no remote copies, remote signals or barrier semaphores. Data moves between devices by JAX's collectives and lax.ppermute only.
A program may use at most 128 MiB of HBM per device.

```python
import math
import jax
import jax.numpy as jnp
import numpy as np
from jax import lax

DW = 3584
FFW = 1024
TOK_DEV = 128
EXPERTS = 32
TOP = 8
CAP = 40
TOKENS = 8192
FRAG = 1024
N_REPLICA = 4
N_DP = 2
N_EXPERT = 32


def levels(rng, shape, shards, low, high):
    loudness = 1.0
    for dim, blocks in shards:
        draws = jax.random.uniform(jax.random.fold_in(jax.random.fold_in(rng, 6), dim), (blocks,), jnp.float32, low / len(shards), high / len(shards))
        loudness = loudness * jnp.repeat(jnp.exp(draws), shape[dim] // blocks).reshape((-1,) + (1,) * (len(shape) - 1 - dim))
    return loudness


def shared_out(stream_key, own, number, rows, count, top, bound, slope):
    order = jax.random.permutation(stream_key, count)
    heavy_load, ordinary = portions_of(count, rows * top, bound, slope, True), portions_of(count, rows * top, bound, slope, False)
    places = jnp.arange(count)

    def named(tallies, turn):
        used = int((tallies > 0).sum())
        fixed = max(1, used // 4)
        moved = fixed + (places - fixed + turn * (used - fixed)) % max(1, count - fixed)
        return jnp.zeros((count,), jnp.int32).at[order[jnp.where(places < fixed, places, moved)]].set(jnp.asarray(tallies, jnp.int32))

    tallies = jnp.where(number % 4 == 0, named(heavy_load, number // 4), named(ordinary, number - number // 4 - 1))
    mixed = jax.random.permutation(jax.random.fold_in(own, 3), count)
    donor, receiver = mixed[0:count // 2 * 2:2], mixed[1:count // 2 * 2:2]
    margin = jnp.minimum(tallies[donor] - 1, bound - tallies[receiver]) // 2
    margin = jnp.where((donor == order[0]) | (receiver == order[0]) | (tallies[receiver] == 0), 0, jnp.maximum(margin, 0))
    moved = jax.random.randint(jax.random.fold_in(own, 4), (count // 2,), 0, 1 << 20) % (margin + 1)
    tallies = tallies.at[donor].add(-moved).at[receiver].add(moved)
    items = jnp.searchsorted(jnp.cumsum(tallies), jnp.arange(rows * top), side="right").astype(jnp.int32)
    table = items.reshape(top, rows).T
    table = table[jax.random.permutation(jax.random.fold_in(own, 1), rows)]
    turn = jax.random.randint(jax.random.fold_in(own, 2), (rows, 1), 0, top)
    return jnp.take_along_axis(table, (jnp.arange(top)[None, :] + turn) % top, axis=1)


def portions_of(count, total, limit, skew, full):
    weights = [(1 << 20) // math.isqrt(standing ** skew) + 1 for standing in range(1, count + 1)]
    largest = limit if full else min(limit, max(-(-total // count), total * weights[0] // sum(weights)))
    least = 1 if total - largest >= count - 1 else 0
    given, rest = [largest] + [least] * (count - 1), total - largest - least * (count - 1)
    while rest > 0:
        free = [i for i in range(1, count) if given[i] < largest] or [i for i in range(1, count) if given[i] < limit]
        mass, remaining = sum([weights[i] for i in free]), rest
        for i in free:
            addition = min(limit - given[i], max(1, remaining * weights[i] // mass), rest)
            given[i] = given[i] + addition
            rest = rest - addition
    return np.array(given)


def scatter_about(key, extent, scale, reach, shards=(), kind=jnp.bfloat16):
    values = jax.random.normal(key, extent, jnp.float32) * scale
    if len(shards) > 0:
        values = levels(key, extent, shards, -0.22, 0.18) * values
    return jnp.clip(values, min=-reach, max=reach).astype(kind)


def setup_inputs(seed: int = 0) -> dict:
    streams_of = jax.random.split(jax.random.key(seed), 8)
    cotangent = scatter_about(streams_of[0], (N_REPLICA, TOKENS, DW), 0.1, 0.59765625, ((0, 4), (1, 64)))
    route_weights = jnp.clip(jnp.exp(math.log(0.5) - 2.3025851 * jax.random.uniform(streams_of[1], (N_REPLICA, TOKENS, TOP), jnp.float32) ** levels(streams_of[1], (N_REPLICA, TOKENS, TOP), ((0, 4), (1, 64)), -0.2, 0.2)), 0.05, 0.5)
    expert_ids_keys = jax.random.split(jax.random.fold_in(streams_of[2], 1), N_REPLICA * TOKENS // TOK_DEV)
    expert_ids_turns = jax.random.permutation(jax.random.fold_in(streams_of[2], 3), N_REPLICA * TOKENS // TOK_DEV)
    expert_ids = jax.vmap(lambda own, number: shared_out(jax.random.fold_in(streams_of[2], 2), own, number, TOK_DEV, EXPERTS, TOP, CAP, 2))(expert_ids_keys, expert_ids_turns).reshape((N_REPLICA, TOKENS, TOP))
    hidden = scatter_about(streams_of[3], (N_REPLICA, EXPERTS, N_DP * N_EXPERT * CAP, FFW), 1.0, 6.0, ((0, 4), (1, 32), (2, 2)))
    local_fragment = scatter_about(streams_of[4], (N_REPLICA, FRAG, DW), 1.0, 6.0, ((0, 4), (1, 64)))
    global_fragment = scatter_about(streams_of[5], (FRAG, DW), 1.0, 6.0, ((0, 64),), jnp.float32)
    outer_momentum = scatter_about(streams_of[6], (FRAG, DW), 0.5, 3.0, ((0, 64),), jnp.float32)
    return {"cotangent": cotangent, "route_weights": route_weights, "expert_ids": expert_ids, "hidden": hidden, "local_fragment": local_fragment, "global_fragment": global_fragment, "outer_momentum": outer_momentum}


def slot_positions(expert_ids):
    blocks = expert_ids.reshape(-1, TOK_DEV * TOP)
    labels = jnp.arange(EXPERTS, dtype=jnp.int32)
    matches = (blocks[:, :, None] == labels[None, None, :]).astype(jnp.int32)
    earlier = jnp.cumsum(matches, axis=1) - matches
    return jnp.sum(earlier * matches, axis=2).astype(jnp.int32).reshape(expert_ids.shape)


def reference(cotangent, route_weights, expert_ids, hidden, local_fragment, global_fragment, outer_momentum):
    slot_index = slot_positions(expert_ids)
    slot_rows = N_DP * N_EXPERT * CAP
    block_index = (jnp.arange(TOKENS, dtype=jnp.int32) // TOK_DEV).astype(jnp.int32)[:, None]

    def per_expert(pieces):
        saved, received = pieces
        product = lax.dot_general(saved, received, (((0,), (0,)), ((), ())), preferred_element_type=jnp.float32)
        return product.astype(jnp.bfloat16)

    def per_replica(pieces):
        grad_rows, weights, routes, slots, saved = pieces
        scaled = (weights[:, :, None] * grad_rows[:, None, :].astype(jnp.float32)).astype(jnp.bfloat16)
        destination = (routes * slot_rows + block_index * CAP + slots).astype(jnp.int32)
        buffer = jnp.zeros((EXPERTS * slot_rows, DW), jnp.bfloat16)
        buffer = buffer.at[destination.reshape(-1)].set(scaled.reshape(-1, DW))
        return lax.map(per_expert, (saved, buffer.reshape(EXPERTS, slot_rows, DW)))

    expert_grad = lax.map(per_replica, (cotangent, route_weights, expert_ids, slot_index, hidden))
    local_now = local_fragment.astype(jnp.float32)
    difference = global_fragment[None, :, :] - local_now
    outer_grad = jnp.sum(difference, axis=0) * (1.0 / N_REPLICA)
    new_momentum = 0.9 * outer_momentum + outer_grad
    new_global = global_fragment - 0.7 * (outer_grad + 0.9 * new_momentum)
    mixed_local = (0.5 * local_now + 0.5 * new_global[None, :, :]).astype(jnp.bfloat16)
    return (expert_grad, new_global, new_momentum, mixed_local)
```

```python
import functools

import jax
import jax.numpy as jnp
from jax import lax
from jax.experimental import pallas as pl
from jax.experimental.pallas import tpu as pltpu
from jax.sharding import Mesh, PartitionSpec as P

Z, Y = 8, 4
TOK, TOP, CAP = 128, 8, 40
VMEM_LIMIT = 40 * 1024 * 1024


def shift(size, step):
    return [(i, (i + step) % size) for i in range(size)]


EXPERT_AT, ZERO_AT = 16, 20


def pick_rows_kernel(count, places, index_ref, *refs):
    tables, blocks, outs = refs[:count], refs[count : 2 * count], refs[2 * count :]
    before = (
        lax.broadcasted_iota(jnp.int32, (TOK, TOK), 0)
        < lax.broadcasted_iota(jnp.int32, (TOK, TOK), 1)
    ).astype(jnp.bfloat16)
    slots = lax.broadcasted_iota(jnp.int32, (CAP, TOK), 0).astype(jnp.float32)
    rows = []
    for table, block in zip(tables, blocks):
        weights, ids = table[0, :TOP], table[0, TOP:]
        hits, gains = [], []
        for j in range(Y):
            hit = ids == index_ref[EXPERT_AT + j].astype(jnp.float32)
            hits.append(jnp.sum(jnp.where(hit, 1.0, 0.0), axis=0, keepdims=True))
            gains.append(jnp.sum(jnp.where(hit, weights, 0.0), axis=0, keepdims=True))
        stacked = jnp.concatenate(hits + hits, axis=0)
        earlier = jnp.dot(stacked.astype(jnp.bfloat16), before, preferred_element_type=jnp.float32)
        earlier = jnp.where(stacked > 0.5, earlier, -1.0)
        chosen, scales = [], []
        for j in range(Y):
            pick = slots == earlier[j : j + 1]
            chosen.append(jnp.where(pick, 1.0, 0.0))
            scales.append(jnp.sum(jnp.where(pick, gains[j], 0.0), axis=1, keepdims=True))
        chosen = jnp.concatenate(chosen, axis=0).astype(jnp.bfloat16)
        taken = jnp.dot(chosen, block[...], preferred_element_type=jnp.float32)
        rows.append(taken * jnp.concatenate(scales, axis=0))
    for j in range(Y):
        parts = [r[j * CAP : (j + 1) * CAP] for r in rows]
        outs[j][...] = jnp.concatenate(parts, axis=0).astype(jnp.bfloat16)


def pick_rows(index, table, places, blocks):
    count, width = len(blocks), blocks[0].shape[1]

    def table_spec(place):
        return pl.BlockSpec((1, 2 * TOP, TOK), lambda i, index: (index[place], 0, 0))

    out = jax.ShapeDtypeStruct((CAP * count, width), jnp.bfloat16)
    return pl.pallas_call(
        functools.partial(pick_rows_kernel, count, places),
        grid_spec=pltpu.PrefetchScalarGridSpec(
            num_scalar_prefetch=1,
            grid=(1,),
            in_specs=[table_spec(p) for p in places]
            + [pl.BlockSpec((TOK, width), lambda i, index: (0, 0))] * count,
            out_specs=[pl.BlockSpec((CAP * count, width), lambda i, index: (0, 0))] * Y,
        ),
        out_shape=[out] * Y,
        compiler_params=pltpu.CompilerParams(vmem_limit_bytes=VMEM_LIMIT),
        cost_estimate=pl.CostEstimate(
            flops=2 * count * Y * CAP * TOK * width,
            bytes_accessed=count * (TOK + Y * CAP) * width * 2,
            transcendentals=0,
        ),
    )(index, *([table] * count), *blocks)


def arrange_kernel(plan, index_ref, *refs):
    sources, out, sems = refs[:-2], refs[-2], refs[-1]
    copies = []
    for i, (which, entry) in enumerate(plan):
        copies.append(
            pltpu.make_async_copy(sources[which].at[index_ref[entry]], out.at[i], sems.at[i])
        )
        copies[-1].start()
    for copy in copies:
        copy.wait()


def arrange(index, sources, plan):
    shape = sources[0].shape
    return pl.pallas_call(
        functools.partial(arrange_kernel, plan),
        in_specs=[pl.BlockSpec(memory_space=pltpu.SMEM)]
        + [pl.BlockSpec(memory_space=pl.ANY)] * len(sources),
        out_specs=pl.BlockSpec(memory_space=pl.ANY),
        out_shape=jax.ShapeDtypeStruct((len(plan),) + shape[1:], sources[0].dtype),
        scratch_shapes=[pltpu.SemaphoreType.DMA((len(plan),))],
        cost_estimate=pl.CostEstimate(
            flops=0, bytes_accessed=len(plan) * CAP * shape[2] * 4, transcendentals=0
        ),
    )(index, *sources)


def accumulate_kernel(sizes, with_total, *refs):
    saved, rest = refs[0], refs[1:]
    if with_total:
        total, rest = rest[0], rest[1:]
    pieces, out, turned = rest[:-2], rest[-2], rest[-1]

    @pl.when(pl.program_id(0) == 0)
    def _():
        turned[...] = saved[...].T

    if min(sizes) % 16:
        rows = jnp.concatenate([p[...].astype(jnp.float32) for p in pieces], axis=0)
        rows = rows.astype(jnp.bfloat16)
    else:
        rows = jnp.concatenate([p[...] for p in pieces], axis=0)
    value = jnp.dot(turned[...], rows, preferred_element_type=jnp.float32)
    if with_total:
        value = value + total[...]
    out[...] = value.astype(out.dtype)


def accumulate(saved, pieces, total, dtype, tile=256):
    depth, hidden = saved.shape
    width = pieces[0].shape[1]
    sizes = tuple(p.shape[0] for p in pieces)
    column = pl.BlockSpec((hidden, tile), lambda n: (0, n))
    totals = [] if total is None else [total]
    return pl.pallas_call(
        functools.partial(accumulate_kernel, sizes, total is not None),
        grid=(width // tile,),
        in_specs=[pl.BlockSpec((depth, hidden), lambda n: (0, 0))]
        + [column] * len(totals)
        + [pl.BlockSpec((s, tile), lambda n: (0, n)) for s in sizes],
        out_specs=column,
        out_shape=jax.ShapeDtypeStruct((hidden, width), dtype),
        scratch_shapes=[pltpu.VMEM((hidden, depth), saved.dtype)],
        compiler_params=pltpu.CompilerParams(vmem_limit_bytes=VMEM_LIMIT),
        cost_estimate=pl.CostEstimate(
            flops=2 * depth * hidden * width,
            bytes_accessed=(4 * hidden + 2 * depth) * width,
            transcendentals=0,
        ),
    )(saved, *totals, *pieces)


def per_device(
    cotangent, route_weights, expert_ids, hidden, local_fragment, global_fragment, outer_momentum
):
    z, y, dp = lax.axis_index("z"), lax.axis_index("y"), lax.axis_index("dp")
    half = cotangent.shape[2] // 2
    down, up, swap = shift(Z, -1), shift(Z, 1), [(0, 1), (1, 0)]
    saved_own = hidden[0, 0]

    other = lax.dynamic_slice(cotangent[0], (0, (1 - dp) * half), (TOK, half))
    peer_block = lax.ppermute(other, "dp", swap)
    own_block = lax.dynamic_slice(cotangent[0], (0, dp * half), (TOK, half))
    own_table = jnp.concatenate(
        [route_weights[0].T, expert_ids[0].T.astype(jnp.float32)], axis=0
    )[None]
    tables = lax.all_gather(own_table, ("dp", "z"), axis=0, tiled=True)
    saved_peer = lax.ppermute(saved_own, "dp", swap)

    offsets = jnp.arange(Z, dtype=jnp.int32)
    ring_z = (z + offsets) % Z
    ring_y = (y + jnp.arange(Y, dtype=jnp.int32)) % Y
    index = jnp.concatenate(
        [dp * Z + ring_z, (1 - dp) * Z + ring_z, z * Y + ring_y, jnp.zeros((1,), jnp.int32)]
    ).astype(jnp.int32)
    piece_index = (ring_z[:, None] * Y + (y - jnp.arange(Y, dtype=jnp.int32))[None, :] % Y).reshape(
        Z * Y
    ).astype(jnp.int32)

    def send(table, places, blocks):
        parts = pick_rows(index, table, places, blocks)
        return [parts[0]] + [lax.ppermute(parts[j], "y", shift(Y, j)) for j in range(1, Y)]

    def plan(offsets, which):
        return [(w, o % Z * Y + j) for j in range(Y) for o, w in zip(offsets, which)]

    own, peer = {0: own_block}, {0: peer_block}
    got = {}
    got["own0"] = send(own_table, (ZERO_AT,), [own_block])
    for k in range(1, 4):
        own[k] = lax.ppermute(own[k - 1], "z", down)
        own[-k] = lax.ppermute(own[1 - k], "z", up)
        got["own", k] = send(tables, (k, Z - k), [own[k], own[-k]])
        if k == 1:
            got["peer0"] = send(tables, (Z,), [peer_block])
        peer[k] = lax.ppermute(peer[k - 1], "z", down)
        peer[-k] = lax.ppermute(peer[1 - k], "z", up)
        got["peer", k] = send(tables, (Z + k, 2 * Z - k), [peer[k], peer[-k]])
    own[4] = lax.ppermute(own[3], "z", down)
    peer[4] = lax.ppermute(peer[-3], "z", up)
    got["far"] = send(tables, (4, Z + 4), [own[4], peer[4]])

    pieces_own = saved_own.reshape(Z * Y, CAP, -1)
    pieces_peer = saved_peer.reshape(Z * Y, CAP, -1)

    def slab(plan):
        return arrange(piece_index, (pieces_own, pieces_peer), plan).reshape(
            len(plan) * CAP, -1
        )

    first = arrange(
        piece_index,
        (pieces_own,),
        plan((0,), (0,)) + plan((1, -1), (0, 0)) + plan((2, -2), (0, 0)),
    ).reshape(20 * CAP, -1)
    second = slab(
        plan((3, -3), (0, 0))
        + plan((0,), (1,))
        + plan((1, -1), (1, 1))
        + plan((2, -2), (1, 1))
    )
    third = slab(plan((3, -3), (1, 1)) + plan((4, 4), (0, 1)))
    total = accumulate(first, got["own0"] + got["own", 1] + got["own", 2], None, jnp.float32)
    total = accumulate(
        second, got["own", 3] + got["peer0"] + got["peer", 1] + got["peer", 2], total, jnp.float32
    )
    gradient = accumulate(third, got["peer", 3] + got["far"], total, jnp.bfloat16)

    replicas = lax.axis_size("xl") * lax.axis_size("core")
    local_now = local_fragment[0]
    difference = global_fragment - local_now.astype(jnp.float32)
    for step in range(1, replicas):
        moved = lax.ppermute(
            local_now, ("xl", "core"), [(i, i ^ step) for i in range(replicas)]
        )
        difference = difference + (global_fragment - moved.astype(jnp.float32))
    outer_grad = difference * (1.0 / replicas)
    new_momentum = 0.9 * outer_momentum + outer_grad
    new_global = global_fragment - 0.7 * (outer_grad + 0.9 * new_momentum)
    mixed_local = (0.5 * local_now.astype(jnp.float32) + 0.5 * new_global).astype(jnp.bfloat16)
    return (gradient[None, None], new_global, new_momentum, mixed_local[None])


def solution(mesh):
    split = Mesh(mesh.devices.reshape(2, 2, 2, Z, Y), ("xl", "core", "dp", "z", "y"))
    replica, expert = ("xl", "core"), ("z", "y")
    rows = ("dp",) + expert
    placed = (
        P(replica, rows, None),
        P(replica, rows, None),
        P(replica, rows, None),
        P(replica, expert, "dp", None),
        P(replica, rows, None),
        P(rows, None),
        P(rows, None),
    )
    return jax.shard_map(
        per_device,
        mesh=split,
        in_specs=placed,
        out_specs=(
            P(replica, expert, None, "dp"),
            P(rows, None),
            P(rows, None),
            P(replica, rows, None),
        ),
        check_vma=False,
    )
```

```python
import functools

import jax
import jax.numpy as jnp
from jax import lax
from jax.experimental import pallas as pl
from jax.experimental.pallas import tpu as pltpu
from jax.sharding import Mesh, PartitionSpec as P

Z, Y = 8, 4
TOK, TOP, CAP = 128, 8, 40
VMEM_LIMIT = 60 * 1024 * 1024


def shift(size, step):
    return [(i, (i + step) % size) for i in range(size)]


HALF_AT, OTHER_AT = 4, 5
TABLE = 128


def picked(index_ref, block):
    width = block.shape[1] - TABLE
    before = (
        lax.broadcasted_iota(jnp.int32, (TOK, TOK), 0)
        < lax.broadcasted_iota(jnp.int32, (TOK, TOK), 1)
    ).astype(jnp.bfloat16)
    slots = lax.broadcasted_iota(jnp.int32, (CAP, TOK), 0).astype(jnp.float32)
    table = block[:, width:].astype(jnp.float32).T
    weights = table[:TOP] + table[TOP : 2 * TOP] + table[2 * TOP : 3 * TOP]
    ids = table[3 * TOP : 4 * TOP]
    hits, gains = [], []
    for j in range(Y):
        hit = ids == index_ref[j].astype(jnp.float32)
        hits.append(jnp.sum(jnp.where(hit, 1.0, 0.0), axis=0, keepdims=True))
        gains.append(jnp.sum(jnp.where(hit, weights, 0.0), axis=0, keepdims=True))
    stacked = jnp.concatenate(hits + hits, axis=0)
    earlier = jnp.dot(stacked.astype(jnp.bfloat16), before, preferred_element_type=jnp.float32)
    earlier = jnp.where(stacked > 0.5, earlier, -1.0)
    chosen, scales = [], []
    for j in range(Y):
        pick = slots == earlier[j : j + 1]
        chosen.append(jnp.where(pick, 1.0, 0.0))
        scales.append(jnp.sum(jnp.where(pick, gains[j], 0.0), axis=1, keepdims=True))
    chosen = jnp.concatenate(chosen, axis=0).astype(jnp.bfloat16)
    taken = jnp.dot(chosen, block[:, :width], preferred_element_type=jnp.float32)
    return taken * jnp.concatenate(scales, axis=0)


def store_rows(index_ref, blocks, outs):
    width = outs[0].shape[1]
    for first in range(0, len(blocks), 2):
        rows = [picked(index_ref, block) for block in blocks[first : first + 2]]
        for j in range(Y):
            parts = [r[j * CAP : (j + 1) * CAP] for r in rows]
            joined = jnp.concatenate(parts, axis=0).astype(jnp.bfloat16)
            for part in range(len(outs) // Y):
                outs[part * Y + j][first * CAP : (first + len(rows)) * CAP] = joined[
                    :, part * width : (part + 1) * width
                ]


def pack_kernel(index_ref, own_ref, other_ref, weights_ref, ids_ref, own_out, other_out):
    del index_ref
    weights = weights_ref[...]
    high = weights.astype(jnp.bfloat16).astype(jnp.float32)
    middle = (weights - high).astype(jnp.bfloat16).astype(jnp.float32)
    low = weights - high - middle
    ids = ids_ref[...].astype(jnp.float32)
    empty = jnp.zeros((TABLE - 4 * TOP, TOK), jnp.float32)
    table = jnp.concatenate([high, middle, low, ids, empty], axis=0).T.astype(jnp.bfloat16)
    width = own_ref.shape[1]
    for block, out in ((own_ref, own_out), (other_ref, other_out)):
        out[:, :width] = block[...]
        out[:, width:] = table


def pack(index, cotangent, weights, ids):
    width = cotangent.shape[1] // 2
    out = jax.ShapeDtypeStruct((TOK, width + TABLE), jnp.bfloat16)
    whole = pl.BlockSpec((TOP, TOK), lambda i, index: (0, 0))
    return pl.pallas_call(
        pack_kernel,
        grid_spec=pltpu.PrefetchScalarGridSpec(
            num_scalar_prefetch=1,
            grid=(1,),
            in_specs=[
                pl.BlockSpec((TOK, width), lambda i, index: (0, index[HALF_AT])),
                pl.BlockSpec((TOK, width), lambda i, index: (0, index[OTHER_AT])),
                whole,
                whole,
            ],
            out_specs=[pl.BlockSpec((TOK, width + TABLE), lambda i, index: (0, 0))] * 2,
        ),
        out_shape=[out] * 2,
        compiler_params=pltpu.CompilerParams(vmem_limit_bytes=VMEM_LIMIT),
        cost_estimate=pl.CostEstimate(
            flops=0, bytes_accessed=8 * TOK * width, transcendentals=0
        ),
    )(index, cotangent, cotangent, weights, ids)


def pick_rows_kernel(count, index_ref, *refs):
    store_rows(index_ref, refs[:count], refs[count:])


def pick_rows(index, *places, halves=1):
    blocks, numbers = zip(*places)
    count, packed = len(blocks), blocks[0].shape[1]
    width = (packed - TABLE) // halves

    def block_spec(number):
        return pl.BlockSpec((TOK, packed), lambda i, index: (number, 0))

    out = jax.ShapeDtypeStruct((CAP * count, width), jnp.bfloat16)
    return pl.pallas_call(
        functools.partial(pick_rows_kernel, count),
        grid_spec=pltpu.PrefetchScalarGridSpec(
            num_scalar_prefetch=1,
            grid=(1,),
            in_specs=[block_spec(number) for number in numbers],
            out_specs=[pl.BlockSpec((CAP * count, width), lambda i, index: (0, 0))] * (Y * halves),
        ),
        out_shape=[out] * (Y * halves),
        compiler_params=pltpu.CompilerParams(vmem_limit_bytes=VMEM_LIMIT),
        cost_estimate=pl.CostEstimate(
            flops=2 * count * Y * CAP * TOK * width * halves,
            bytes_accessed=count * (TOK + Y * CAP) * width * halves * 2,
            transcendentals=0,
        ),
    )(index, *blocks)


def arrange_kernel(plans, sources, index_ref, *refs):
    for plan, out in zip(plans, refs[sources:]):
        for i in range(0, len(plan), 2):
            pair = [refs[g][index_ref[at]].astype(jnp.float32) for g, at in plan[i : i + 2]]
            out[i * CAP : (i + 2) * CAP] = jnp.concatenate(pair, axis=0).astype(jnp.bfloat16)


def arrange(index, sources, plans, tile=256):
    hidden = sources[0].shape[2]
    depths = [CAP * len(plan) for plan in plans]
    return pl.pallas_call(
        functools.partial(arrange_kernel, plans, len(sources)),
        grid_spec=pltpu.PrefetchScalarGridSpec(
            num_scalar_prefetch=1,
            grid=(hidden // tile,),
            in_specs=[
                pl.BlockSpec((s.shape[0], CAP, tile), lambda m, index: (0, 0, m)) for s in sources
            ],
            out_specs=[pl.BlockSpec((d, tile), lambda m, index: (0, m)) for d in depths],
        ),
        out_shape=[jax.ShapeDtypeStruct((d, hidden), jnp.bfloat16) for d in depths],
        compiler_params=pltpu.CompilerParams(vmem_limit_bytes=VMEM_LIMIT),
        cost_estimate=pl.CostEstimate(
            flops=0, bytes_accessed=4 * sum(depths) * hidden, transcendentals=0
        ),
    )(index, *sources)


def joined_rows(part, pieces, columns):
    rows = []
    for first in range(0, len(part), 2):
        pair = [pieces[at][low:high, columns] for at, low, high in part[first : first + 2]]
        if pair[0].shape[0] % 16:
            joined = jnp.concatenate([p.astype(jnp.float32) for p in pair], axis=0)
            rows.append(joined.astype(jnp.bfloat16))
        else:
            rows.extend(pair)
    return jnp.concatenate(rows, axis=0)


def outer_products(saved, rows):
    return lax.dot_general(saved, rows, (((0,), (0,)), ((), ())), preferred_element_type=jnp.float32)


def accumulate_kernel(part, with_total, saved, *refs):
    pieces, out = refs[with_total:-1], refs[-1]
    size = out.shape[1]
    columns = pl.ds(pl.multiple_of(pl.program_id(0) * size, size), size)
    value = outer_products(saved[...], joined_rows(part, pieces, columns))
    if with_total:
        value = value + refs[0][...]
    out[...] = value.astype(out.dtype)


def accumulate(saved, part, pieces, total, dtype, tile=896):
    depth, hidden = saved.shape
    width = pieces[0].shape[1]
    column = pl.BlockSpec((hidden, tile), lambda n: (0, n))
    totals = [] if total is None else [total]

    def whole(array):
        return pl.BlockSpec(array.shape, lambda n: (0, 0))

    return pl.pallas_call(
        functools.partial(accumulate_kernel, part, len(totals)),
        grid=(width // tile,),
        in_specs=[whole(saved)] + [column] * len(totals) + [whole(p) for p in pieces],
        out_specs=column,
        out_shape=jax.ShapeDtypeStruct((hidden, width), dtype),
        compiler_params=pltpu.CompilerParams(vmem_limit_bytes=VMEM_LIMIT),
        cost_estimate=pl.CostEstimate(
            flops=2 * depth * hidden * width,
            bytes_accessed=(4 * hidden + 2 * depth) * width,
            transcendentals=0,
        ),
    )(saved, *totals, *pieces)


def per_device(
    cotangent, route_weights, expert_ids, hidden, local_fragment, global_fragment, outer_momentum
):
    z, y, dp = lax.axis_index("z"), lax.axis_index("y"), lax.axis_index("dp")
    down, up, swap = shift(Z, -1), shift(Z, 1), [(0, 1), (1, 0)]

    ring_z = (z + jnp.arange(Z, dtype=jnp.int32)) % Z
    ring_y = (y + jnp.arange(Y, dtype=jnp.int32)) % Y
    index = jnp.concatenate([z * Y + ring_y, jnp.stack([dp, 1 - dp])]).astype(jnp.int32)
    senders = (y - jnp.arange(Y, dtype=jnp.int32)) % Y
    ring = (ring_z[:, None] * Y + senders[None, :]).reshape(Z * Y).astype(jnp.int32)

    def plan(offsets, groups):
        return [(g, o % Z * Y + j) for j in range(Y) for o, g in zip(offsets, groups)]

    def after(done, *waiting):
        held = lax.optimization_barrier((*done, *waiting))
        return list(held[len(done) :])

    own_block, other_block = pack(index, cotangent[0], route_weights[0].T, expert_ids[0].T)
    peer_block = lax.ppermute(other_block, "dp", swap)
    (saved_sent,) = after([own_block], hidden[0, 0])
    saved_peer = lax.ppermute(saved_sent, "dp", swap)
    saved = [hidden[0, 0].reshape(Z * Y, CAP, -1), saved_peer.reshape(Z * Y, CAP, -1)]

    def send(parts, earlier=None):
        got = {0: parts[0]}
        for j in (1, 3, 2):
            part = parts[j]
            if earlier is not None:
                (part,) = after([earlier[j]], part)
            got[j] = lax.ppermute(part, "y", shift(Y, j))
        return [got[j] for j in range(Y)]

    def step(blocks):
        return lax.ppermute(blocks[0], "z", down), lax.ppermute(blocks[1], "z", up)

    own_1 = step((own_block, own_block))
    parts = pick_rows(index, (own_1[0], 0), (own_1[1], 0), (own_block, 0), (peer_block, 0))
    round_1 = step([jnp.concatenate([peer_block, block], axis=0) for block in own_1])
    rows_a = send(parts)
    parts = pick_rows(index, *[(r, 1) for r in round_1], *[(r, 0) for r in round_1])
    round_2 = step(after([rows_a[1], rows_a[3]], *round_1))
    rows_b = send(parts, rows_a)
    parts = pick_rows(index, *[(r, 1) for r in round_2], *[(r, 0) for r in round_2])
    round_3 = step(after([rows_a[2], rows_b[1], rows_b[3], saved_peer], *round_2))
    rows_c = send(parts, rows_b)
    (last,) = after([rows_b[2]], round_3[0][:TOK])
    peer_4 = lax.ppermute(last, "z", down)
    saved_early, saved_last = arrange(
        ring,
        saved,
        [
            plan((1, -1, 0, 0), (0, 0, 0, 1))
            + plan((2, -2, 1, -1), (0, 0, 1, 1))
            + plan((3, -3, 2, -2), (0, 0, 1, 1)),
            plan((3, -3, 4, 4), (1, 1, 0, 1)),
        ],
    )
    (peer_4,) = after([rows_c[1], rows_c[3], saved_early], peer_4)
    parts = pick_rows(index, (round_3[0], 0), (round_3[1], 0), (round_3[0], 1), (peer_4, 0))
    rows_d = send(parts, rows_c)

    (local_sent,) = after(parts[:1], local_fragment[0])
    local_now = local_fragment[0].astype(jnp.float32)
    other_core = lax.ppermute(local_sent, "core", swap).astype(jnp.float32)
    difference = (global_fragment - local_now) + (global_fragment - other_core)
    difference = difference + lax.ppermute(difference, "xl", swap)

    def rows(stage):
        return [(stage * Y + j, 0, 4 * CAP) for j in range(Y)]

    (saved_early,) = after(parts[:1], saved_early)
    total = accumulate(
        saved_early, rows(0) + rows(1) + rows(2), rows_a + rows_b + rows_c, None, jnp.float32
    )
    gradient = accumulate(saved_last, rows(0), rows_d, total, jnp.bfloat16)

    replicas = lax.axis_size("xl") * lax.axis_size("core")
    outer_grad = difference * (1.0 / replicas)
    new_momentum = 0.9 * outer_momentum + outer_grad
    new_global = global_fragment - 0.7 * (outer_grad + 0.9 * new_momentum)
    mixed_local = (0.5 * local_now + 0.5 * new_global).astype(jnp.bfloat16)
    return (gradient[None, None], new_global, new_momentum, mixed_local[None])


def solution(mesh):
    split = Mesh(mesh.devices.reshape(2, 2, 2, Z, Y), ("xl", "core", "dp", "z", "y"))
    replica, expert = ("xl", "core"), ("z", "y")
    rows = ("dp",) + expert
    placed = (
        P(replica, rows, None),
        P(replica, rows, None),
        P(replica, rows, None),
        P(replica, expert, "dp", None),
        P(replica, rows, None),
        P(rows, None),
        P(rows, None),
    )
    return jax.shard_map(
        per_device,
        mesh=split,
        in_specs=placed,
        out_specs=(
            P(replica, expert, None, "dp"),
            P(rows, None),
            P(rows, None),
            P(replica, rows, None),
        ),
        check_vma=False,
    )
```

```python
import functools

import jax
import jax.numpy as jnp
from jax import lax
from jax.experimental import pallas as pl
from jax.experimental.pallas import tpu as pltpu
from jax.sharding import Mesh, PartitionSpec as P

Z, Y = 8, 4
TOK, TOP, CAP = 128, 8, 40
VMEM_LIMIT = 63 * 1024 * 1024
PICK_VMEM = 20 * 1024 * 1024


def shift(size, step):
    return [(i, (i + step) % size) for i in range(size)]


HALF_AT, OTHER_AT, PIECES_AT = 4, 5, 8
TABLE = 128


def picked(index_ref, block):
    width = block.shape[1] - TABLE
    before = (
        lax.broadcasted_iota(jnp.int32, (TOK, TOK), 0)
        < lax.broadcasted_iota(jnp.int32, (TOK, TOK), 1)
    ).astype(jnp.bfloat16)
    slots = lax.broadcasted_iota(jnp.int32, (CAP, TOK), 0).astype(jnp.float32)
    table = block[:, width:].astype(jnp.float32).T
    weights = table[:TOP] + table[TOP : 2 * TOP] + table[2 * TOP : 3 * TOP]
    ids = table[3 * TOP : 4 * TOP]
    hits, gains = [], []
    for j in range(Y):
        hit = ids == index_ref[j].astype(jnp.float32)
        hits.append(jnp.sum(jnp.where(hit, 1.0, 0.0), axis=0, keepdims=True))
        gains.append(jnp.sum(jnp.where(hit, weights, 0.0), axis=0, keepdims=True))
    stacked = jnp.concatenate(hits + hits, axis=0)
    earlier = jnp.dot(stacked.astype(jnp.bfloat16), before, preferred_element_type=jnp.float32)
    earlier = jnp.where(stacked > 0.5, earlier, -1.0)
    chosen, scales = [], []
    for j in range(Y):
        pick = slots == earlier[j : j + 1]
        chosen.append(jnp.where(pick, 1.0, 0.0))
        scales.append(jnp.sum(jnp.where(pick, gains[j], 0.0), axis=1, keepdims=True))
    chosen = jnp.concatenate(chosen, axis=0).astype(jnp.bfloat16)
    taken = jnp.dot(chosen, block[:, :width], preferred_element_type=jnp.float32)
    return taken * jnp.concatenate(scales, axis=0)


def store_rows(index_ref, blocks, outs):
    width = outs[0].shape[1]
    for first in range(0, len(blocks), 2):
        rows = [picked(index_ref, block) for block in blocks[first : first + 2]]
        for j in range(Y):
            parts = [r[j * CAP : (j + 1) * CAP] for r in rows]
            joined = jnp.concatenate(parts, axis=0).astype(jnp.bfloat16)
            for part in range(len(outs) // Y):
                outs[part * Y + j][first * CAP : (first + len(rows)) * CAP] = joined[
                    :, part * width : (part + 1) * width
                ]


def pack_kernel(index_ref, own_ref, other_ref, weights_ref, ids_ref, own_out, other_out):
    del index_ref
    weights = weights_ref[...]
    high = weights.astype(jnp.bfloat16).astype(jnp.float32)
    middle = (weights - high).astype(jnp.bfloat16).astype(jnp.float32)
    low = weights - high - middle
    ids = ids_ref[...].astype(jnp.float32)
    empty = jnp.zeros((TABLE - 4 * TOP, TOK), jnp.float32)
    table = jnp.concatenate([high, middle, low, ids, empty], axis=0).T.astype(jnp.bfloat16)
    width = own_ref.shape[1]
    for block, out in ((own_ref, own_out), (other_ref, other_out)):
        out[:, :width] = block[...]
        out[:, width:] = table


def pack(index, cotangent, weights, ids):
    width = cotangent.shape[1] // 2
    out = jax.ShapeDtypeStruct((TOK, width + TABLE), jnp.bfloat16)
    whole = pl.BlockSpec((TOP, TOK), lambda i, index: (0, 0))
    return pl.pallas_call(
        pack_kernel,
        grid_spec=pltpu.PrefetchScalarGridSpec(
            num_scalar_prefetch=1,
            grid=(1,),
            in_specs=[
                pl.BlockSpec((TOK, width), lambda i, index: (0, index[HALF_AT])),
                pl.BlockSpec((TOK, width), lambda i, index: (0, index[OTHER_AT])),
                whole,
                whole,
            ],
            out_specs=[pl.BlockSpec((TOK, width + TABLE), lambda i, index: (0, 0))] * 2,
        ),
        out_shape=[out] * 2,
        compiler_params=pltpu.CompilerParams(vmem_limit_bytes=VMEM_LIMIT),
        cost_estimate=pl.CostEstimate(
            flops=0, bytes_accessed=8 * TOK * width, transcendentals=0
        ),
    )(index, cotangent, cotangent, weights, ids)


def pick_rows_kernel(count, index_ref, *refs):
    store_rows(index_ref, refs[:count], refs[count:])


def pick_rows(index, *places, halves=1):
    blocks, numbers = zip(*places)
    count, packed = len(blocks), blocks[0].shape[1]
    width = (packed - TABLE) // halves

    def block_spec(number):
        return pl.BlockSpec((TOK, packed), lambda i, index: (number, 0))

    out = jax.ShapeDtypeStruct((CAP * count, width), jnp.bfloat16)
    return pl.pallas_call(
        functools.partial(pick_rows_kernel, count),
        grid_spec=pltpu.PrefetchScalarGridSpec(
            num_scalar_prefetch=1,
            grid=(1,),
            in_specs=[block_spec(number) for number in numbers],
            out_specs=[pl.BlockSpec((CAP * count, width), lambda i, index: (0, 0))] * (Y * halves),
        ),
        out_shape=[out] * (Y * halves),
        compiler_params=pltpu.CompilerParams(vmem_limit_bytes=PICK_VMEM),
        cost_estimate=pl.CostEstimate(
            flops=2 * count * Y * CAP * TOK * width * halves,
            bytes_accessed=count * (TOK + Y * CAP) * width * halves * 2,
            transcendentals=0,
        ),
    )(index, *blocks)


def arrange_kernel(plans, sources, index_ref, *refs):
    for plan, out in zip(plans, refs[sources:]):
        for i in range(0, len(plan), 2):
            pair = [refs[g][index_ref[at]].astype(jnp.float32) for g, at in plan[i : i + 2]]
            out[i * CAP : (i + 2) * CAP] = jnp.concatenate(pair, axis=0).astype(jnp.bfloat16)


def arrange(index, sources, plans, tile=256):
    hidden = sources[0].shape[2]
    depths = [CAP * len(plan) for plan in plans]
    return pl.pallas_call(
        functools.partial(arrange_kernel, plans, len(sources)),
        grid_spec=pltpu.PrefetchScalarGridSpec(
            num_scalar_prefetch=1,
            grid=(hidden // tile,),
            in_specs=[
                pl.BlockSpec((s.shape[0], CAP, tile), lambda m, index: (0, 0, m)) for s in sources
            ],
            out_specs=[pl.BlockSpec((d, tile), lambda m, index: (0, m)) for d in depths],
        ),
        out_shape=[jax.ShapeDtypeStruct((d, hidden), jnp.bfloat16) for d in depths],
        compiler_params=pltpu.CompilerParams(vmem_limit_bytes=VMEM_LIMIT),
        cost_estimate=pl.CostEstimate(
            flops=0, bytes_accessed=4 * sum(depths) * hidden, transcendentals=0
        ),
    )(index, *sources)


def joined_rows(part, pieces, columns):
    rows = []
    for first in range(0, len(part), 2):
        pair = [pieces[at][low:high, columns] for at, low, high in part[first : first + 2]]
        if pair[0].shape[0] % 16:
            joined = jnp.concatenate([p.astype(jnp.float32) for p in pair], axis=0)
            rows.append(joined.astype(jnp.bfloat16))
        else:
            rows.extend(pair)
    return jnp.concatenate(rows, axis=0)


def outer_products(saved, rows):
    return lax.dot_general(saved, rows, (((0,), (0,)), ((), ())), preferred_element_type=jnp.float32)


def accumulate_kernel(part, with_total, saved, *refs):
    pieces, out = refs[with_total:-1], refs[-1]
    size = out.shape[1]
    columns = pl.ds(pl.multiple_of(pl.program_id(0) * size, size), size)
    value = outer_products(saved[...], joined_rows(part, pieces, columns))
    if with_total:
        value = value + refs[0][...]
    out[...] = value.astype(out.dtype)


def accumulate(saved, part, pieces, total, dtype, tile=896):
    depth, hidden = saved.shape
    width = pieces[0].shape[1]
    column = pl.BlockSpec((hidden, tile), lambda n: (0, n))
    totals = [] if total is None else [total]

    def whole(array):
        return pl.BlockSpec(array.shape, lambda n: (0, 0))

    return pl.pallas_call(
        functools.partial(accumulate_kernel, part, len(totals)),
        grid=(width // tile,),
        in_specs=[whole(saved)] + [column] * len(totals) + [whole(p) for p in pieces],
        out_specs=column,
        out_shape=jax.ShapeDtypeStruct((hidden, width), dtype),
        compiler_params=pltpu.CompilerParams(vmem_limit_bytes=VMEM_LIMIT),
        cost_estimate=pl.CostEstimate(
            flops=2 * depth * hidden * width,
            bytes_accessed=(4 * hidden + 2 * depth) * width,
            transcendentals=0,
        ),
    )(saved, *totals, *pieces)


def per_device(
    cotangent, route_weights, expert_ids, hidden, local_fragment, global_fragment, outer_momentum
):
    z, y, dp = lax.axis_index("z"), lax.axis_index("y"), lax.axis_index("dp")
    down, up, swap = shift(Z, -1), shift(Z, 1), [(0, 1), (1, 0)]

    place = jnp.arange(PIECES_AT + Z * Y, dtype=jnp.int32)
    offset, sender = (place - PIECES_AT) // Y, place - PIECES_AT
    piece = ((z + offset) & (Z - 1)) * Y + ((y - sender) & (Y - 1))
    index = jnp.where(
        place < HALF_AT,
        z * Y + ((y + place) & (Y - 1)),
        jnp.where(place < PIECES_AT, (dp + place - HALF_AT) & 1, piece),
    )

    def plan(offsets, groups):
        return [(g, PIECES_AT + o % Z * Y + j) for j in range(Y) for o, g in zip(offsets, groups)]

    def after(done, *waiting):
        held = lax.optimization_barrier((*done, *waiting))
        return list(held[len(done) :])

    own_block, other_block = pack(index, cotangent[0], route_weights[0].T, expert_ids[0].T)
    peer_block = lax.ppermute(other_block, "dp", swap)
    (saved_sent,) = after([own_block], hidden[0, 0])
    saved_peer = lax.ppermute(saved_sent, "dp", swap)
    saved = [hidden[0, 0].reshape(Z * Y, CAP, -1), saved_peer.reshape(Z * Y, CAP, -1)]

    def send(parts, earlier=None):
        got = {0: parts[0]}
        for j in (1, 3, 2):
            part = parts[j]
            if earlier is not None:
                (part,) = after([earlier[j]], part)
            got[j] = lax.ppermute(part, "y", shift(Y, j))
        return [got[j] for j in range(Y)]

    def step(blocks):
        return lax.ppermute(blocks[0], "z", down), lax.ppermute(blocks[1], "z", up)

    own_1 = step((own_block, own_block))
    parts = pick_rows(index, (own_1[0], 0), (own_1[1], 0), (own_block, 0), (peer_block, 0))
    round_1 = step([jnp.concatenate([peer_block, block], axis=0) for block in own_1])
    rows_a = send(parts)
    parts = pick_rows(index, *[(r, 1) for r in round_1], *[(r, 0) for r in round_1])
    round_2 = step(after([rows_a[1], rows_a[3]], *round_1))
    rows_b = send(parts, rows_a)
    parts = pick_rows(index, *[(r, 1) for r in round_2], *[(r, 0) for r in round_2])
    round_3 = step(after([rows_a[2], rows_b[1], rows_b[3], saved_peer], *round_2))
    rows_c = send(parts, rows_b)
    saved_early, saved_last = arrange(
        index,
        saved,
        [
            plan((1, -1, 0, 0), (0, 0, 0, 1))
            + plan((2, -2, 1, -1), (0, 0, 1, 1))
            + plan((3, -3, 2, -2), (0, 0, 1, 1)),
            plan((3, -3, 4, 4), (1, 1, 0, 1)),
        ],
    )
    (last,) = after([rows_b[2], saved_early], round_3[0][:TOK])
    peer_4 = lax.ppermute(last, "z", down)
    (peer_4,) = after([rows_c[1], rows_c[3]], peer_4)
    parts = pick_rows(index, (round_3[0], 0), (round_3[1], 0), (round_3[0], 1), (peer_4, 0))
    rows_d = send(parts, rows_c)

    (local_sent,) = after(parts[:1], local_fragment[0])
    local_now = local_fragment[0].astype(jnp.float32)
    other_core = lax.ppermute(local_sent, "core", swap).astype(jnp.float32)
    difference = (global_fragment - local_now) + (global_fragment - other_core)
    difference = difference + lax.ppermute(difference, "xl", swap)

    def rows(stage):
        return [(stage * Y + j, 0, 4 * CAP) for j in range(Y)]

    (saved_early,) = after(parts[:1], saved_early)
    total = accumulate(
        saved_early, rows(0) + rows(1) + rows(2), rows_a + rows_b + rows_c, None, jnp.float32
    )
    gradient = accumulate(saved_last, rows(0), rows_d, total, jnp.bfloat16)

    replicas = lax.axis_size("xl") * lax.axis_size("core")
    outer_grad = difference * (1.0 / replicas)
    new_momentum = 0.9 * outer_momentum + outer_grad
    new_global = global_fragment - 0.7 * (outer_grad + 0.9 * new_momentum)
    mixed_local = (0.5 * local_now + 0.5 * new_global).astype(jnp.bfloat16)
    return (gradient[None, None], new_global, new_momentum, mixed_local[None])


def solution(mesh):
    split = Mesh(mesh.devices.reshape(2, 2, 2, Z, Y), ("xl", "core", "dp", "z", "y"))
    replica, expert = ("xl", "core"), ("z", "y")
    rows = ("dp",) + expert
    placed = (
        P(replica, rows, None),
        P(replica, rows, None),
        P(replica, rows, None),
        P(replica, expert, "dp", None),
        P(replica, rows, None),
        P(rows, None),
        P(rows, None),
    )
    return jax.shard_map(
        per_device,
        mesh=split,
        in_specs=placed,
        out_specs=(
            P(replica, expert, None, "dp"),
            P(rows, None),
            P(rows, None),
            P(replica, rows, None),
        ),
        check_vma=False,
    )
```
